32 devices in a mesh: ctx: 8 (over z, core), wa: 4 (over y, x).
Axes of the slice: x: 2, y: 2, z: 4, core: 2. Of those that a mesh axis runs over, the one named last changes fastest.
Arguments:
- hidden_in: bfloat16 [4096, 576], P('ctx'), may hold values from -6 to 6
- pair_table: int32 [16], replicated, may hold values from 0 to 15, each once
- norm1_gain: bfloat16 [2, 576], replicated, may hold values from 0.099609375 to 1.8984375
- qkv_weight: bfloat16 [2, 576, 960], P(None, 'wa'), may hold values from -0.25 to 0.25
- out_weight: bfloat16 [2, 576, 576], P(None, 'wa'), may hold values from -4 to 4
- norm2_gain: bfloat16 [2, 576], replicated, may hold values from 0.099609375 to 1.8984375
- gate_up_weight: bfloat16 [2, 2, 576, 1536], P(None, None, None, 'wa'), may hold values from -0.25 to 0.25
- down_weight: bfloat16 [2, 1536, 576], P(None, 'wa'), may hold values from -0.15625 to 0.15625
- out_grad: bfloat16 [4096, 576], P('ctx'), may hold values from -6 to 6
Outputs:
- hidden_out: float32 [4096, 576], P('ctx')
- input_grad: float32 [4096, 576], P('ctx')
- norm1_gain_grad: float32 [2, 576], replicated
- qkv_weight_grad: float32 [2, 576, 960], P(None, 'wa')
- out_weight_grad: float32 [2, 576, 576], P(None, 'wa')
- norm2_gain_grad: float32 [2, 576], replicated
- gate_up_weight_grad: float32 [2, 2, 576, 1536], P(None, None, None, 'wa')
- down_weight_grad: float32 [2, 1536, 576], P(None, 'wa')
The draws below stay inside these ranges and needn't reach their ends.
Inputs may be any that keep to these rules, and one draw needn't show every extreme that they name: `pair_table`: each pair number stands once; slot s lies on index s // 2 of ctx.
All inputs are finite; a program needn't handle non-finite values.
Results may differ from the reference program's by a relative error of at most 0.04.
Values may be sent and summed in bfloat16 or wider, within the bound.
A program may use at most 128 MiB of HBM per device.

```python
import jax
import jax.numpy as jnp
from jax import lax

D = 576
QUERY_HEADS = 9
KEY_VALUE_HEADS = 3
HEAD_SIZE = 64
FF = 1536
BLK = 128
LAYERS = 2
QKVW = 960
NPAIRS = 16
SEQ = 4096


def block_scale(stream_key, dims, split, smallest, high):
    def one(axis_at, shards_of):
        heights = jax.random.uniform(jax.random.fold_in(jax.random.fold_in(stream_key, 6), axis_at), (shards_of,), jnp.float32, smallest / len(split), high / len(split))
        return jnp.repeat(jnp.exp(heights), dims[axis_at] // shards_of).reshape((-1,) + (1,) * (len(dims) - axis_at - 1))

    factor_of = one(*split[0])
    for cut in split[1:]:
        factor_of = factor_of * one(*cut)
    return factor_of


def bell_draw(rng, dims, spread, reach, shards=(), kind=jnp.bfloat16):
    drawn = jax.random.normal(rng, dims, jnp.float32) * spread
    if len(shards) > 0:
        drawn = block_scale(rng, dims, shards, -0.22, 0.18) * drawn
    return jnp.clip(drawn, min=-reach, max=reach).astype(kind)


def setup_inputs(seed: int = 0) -> dict:
    arg_keys = jax.random.split(jax.random.key(seed), 10)
    return {
        "hidden_in": bell_draw(arg_keys[0], (SEQ, D), 1.0, 6.0, ((0, 8),)),
        "pair_table": jax.random.permutation(arg_keys[1], NPAIRS).astype(jnp.int32),
        "norm1_gain": jnp.clip(1.0 + 0.18 * jax.random.normal(arg_keys[2], (LAYERS, D), jnp.float32), 0.099609375, 1.8984375).astype(jnp.bfloat16),
        "qkv_weight": bell_draw(arg_keys[3], (LAYERS, D, QKVW), D ** -0.5, 0.25, ((1, 4),)),
        "out_weight": bell_draw(arg_keys[4], (LAYERS, D, D), (D * 16 * SEQ ** -1) ** -0.5, 4.0, ((1, 4),)),
        "norm2_gain": jnp.clip(1.0 + 0.18 * jax.random.normal(arg_keys[5], (LAYERS, D), jnp.float32), 0.099609375, 1.8984375).astype(jnp.bfloat16),
        "gate_up_weight": bell_draw(arg_keys[6], (LAYERS, 2, D, FF), D ** -0.5, 0.25, ((3, 4),)),
        "down_weight": bell_draw(arg_keys[7], (LAYERS, FF, D), FF ** -0.5, 0.15625, ((1, 4),)),
        "out_grad": bell_draw(arg_keys[8], (SEQ, D), 1.0, 6.0, ((0, 8),)),
    }


EPSILON = 1e-05
HIGHEST = lax.Precision.HIGHEST

@jax.custom_vjp
def low(v):
    return lax.optimization_barrier(v.astype(jnp.bfloat16)).astype(jnp.float32)

@jax.custom_vjp
def low_back(v):
    return v

def low_keep(v):
    return (low(v), None)

def low_pass(kept, grad):
    return (grad,)

def back_keep(v):
    return (v, None)

def back_low(kept, grad):
    return (low(grad),)
low.defvjp(low_keep, low_pass)
low_back.defvjp(back_keep, back_low)

def positions(pair_table):
    block_seq = jnp.stack([pair_table, 2 * NPAIRS - 1 - pair_table], axis=1).reshape(-1)
    offsets = jnp.arange(BLK, dtype=jnp.int32)
    return (block_seq[:, None] * BLK + offsets[None, :]).reshape(-1).astype(jnp.int32)

def rotation(token_pos, head_width):
    half_width = head_width // 2
    inv_freq = jnp.power(jnp.float32(100000.0), -2.0 * jnp.arange(half_width, dtype=jnp.float32) / head_width)
    angles = token_pos.astype(jnp.float32)[..., None] * inv_freq
    return (jnp.cos(angles), jnp.sin(angles))

def apply_rotary(vectors, cosine, sine):
    half_width = vectors.shape[-1] // 2
    first_half = vectors[..., :half_width]
    second_half = vectors[..., half_width:]
    cosine = cosine[..., None, :]
    sine = sine[..., None, :]
    return jnp.concatenate([first_half * cosine - second_half * sine, second_half * cosine + first_half * sine], axis=-1)

def dense(left, right):
    return jnp.dot(left, right, precision=HIGHEST, preferred_element_type=jnp.float32)

def attend(query_rows, key_matrix_rows, value_matrix_rows, token_pos):
    sequence_length = query_rows.shape[0]
    block_length = min(512, sequence_length)
    head_cluster = QUERY_HEADS // KEY_VALUE_HEADS
    score_scale = HEAD_SIZE ** (-0.5)
    query_block_list = query_rows.reshape(sequence_length // block_length, block_length, KEY_VALUE_HEADS, head_cluster, HEAD_SIZE)
    pos_blocks = token_pos.reshape(sequence_length // block_length, block_length)

    def one_block(pieces):
        query_blk, query_pos = pieces
        scores = low_back(jnp.einsum('qgrd,kgd->grqk', query_blk, key_matrix_rows, precision=HIGHEST))
        live = token_pos[None, None, None, :] <= query_pos[None, None, :, None]
        scaled = jnp.where(live, scores * score_scale, -1e+30)
        row_max = lax.optimization_barrier(jnp.max(scaled, axis=-1, keepdims=True))
        exponent = jnp.exp(scaled - row_max)
        probability = low(exponent / lax.optimization_barrier(jnp.sum(exponent, axis=-1, keepdims=True)))
        return jnp.einsum('grqk,kgd->qgrd', probability, value_matrix_rows, precision=HIGHEST)
    outputs = lax.map(jax.checkpoint(one_block), (query_block_list, pos_blocks))
    return outputs.reshape(sequence_length, QUERY_HEADS * HEAD_SIZE)

def forward(hidden, norm1_gain, qkv_weight, out_weight, norm2_gain, gate_up_weight, down_weight, token_pos):
    sequence_length = hidden.shape[0]
    cosine, sine = rotation(token_pos, HEAD_SIZE)
    for layer_at in range(LAYERS):
        inv_one = lax.rsqrt(lax.optimization_barrier(jnp.mean(hidden * hidden, axis=-1, keepdims=True)) + EPSILON)
        normed = low(hidden * inv_one * norm1_gain[layer_at])
        combined_parts = low_back(dense(normed, qkv_weight[layer_at]))
        query_rows = combined_parts[:, :QUERY_HEADS * HEAD_SIZE].reshape(sequence_length, QUERY_HEADS, HEAD_SIZE)
        key_matrix_rows = combined_parts[:, QUERY_HEADS * HEAD_SIZE:(QUERY_HEADS + KEY_VALUE_HEADS) * HEAD_SIZE].reshape(sequence_length, KEY_VALUE_HEADS, HEAD_SIZE)
        value_matrix_rows = combined_parts[:, (QUERY_HEADS + KEY_VALUE_HEADS) * HEAD_SIZE:].reshape(sequence_length, KEY_VALUE_HEADS, HEAD_SIZE)
        query_rows = low(apply_rotary(query_rows, cosine, sine))
        key_matrix_rows = low(apply_rotary(key_matrix_rows, cosine, sine))
        value_matrix_rows = low(value_matrix_rows)
        attended = low_back(low(attend(query_rows, key_matrix_rows, value_matrix_rows, token_pos)))
        middle = hidden + low_back(dense(attended, out_weight[layer_at]))
        inv_two = lax.rsqrt(lax.optimization_barrier(jnp.mean(middle * middle, axis=-1, keepdims=True)) + EPSILON)
        normed_two = low(middle * inv_two * norm2_gain[layer_at])
        gate_pre = low_back(dense(normed_two, gate_up_weight[layer_at, 0]))
        up_proj = low_back(dense(normed_two, gate_up_weight[layer_at, 1]))
        activated = low(jax.nn.silu(gate_pre) * up_proj)
        hidden = middle + low_back(dense(activated, down_weight[layer_at]))
    return hidden

def reference(hidden_in, pair_table, norm1_gain, qkv_weight, out_weight, norm2_gain, gate_up_weight, down_weight, out_grad):
    token_pos = positions(pair_table)
    floats = (hidden_in.astype(jnp.float32), norm1_gain.astype(jnp.float32), qkv_weight.astype(jnp.float32), out_weight.astype(jnp.float32), norm2_gain.astype(jnp.float32), gate_up_weight.astype(jnp.float32), down_weight.astype(jnp.float32))

    def network(hidden, gain_one, weight_qkv, weight_out, gain_two, weight_gate_up, weight_down):
        return forward(hidden, gain_one, weight_qkv, weight_out, gain_two, weight_gate_up, weight_down, token_pos)
    hidden_out, pullback = jax.vjp(network, *floats)
    grads = pullback(out_grad.astype(jnp.float32))
    return (hidden_out, grads[0], grads[1], grads[2], grads[3], grads[4], grads[5], grads[6])
```

```python
import functools

import jax
import jax.numpy as jnp
from jax import lax
from jax.experimental import pallas as pl
from jax.experimental.pallas import tpu as pltpu
from jax.sharding import PartitionSpec as P

QUERY_HEADS = 9
KEY_VALUE_HEADS = 3
HEAD_SIZE = 64
BLK = 128
LAYERS = 2


EPSILON = 1e-05
KEY_CHUNK = 512
VMEM_BYTES = 50 * 1024 * 1024


def rotation(token_pos, head_width):
    half_width = head_width // 2
    inv_freq = jnp.power(
        jnp.float32(100000.0), -2.0 * jnp.arange(half_width, dtype=jnp.float32) / head_width
    )
    angles = token_pos.astype(jnp.float32)[..., None] * inv_freq
    return (jnp.cos(angles), jnp.sin(angles))


def apply_rotary(vectors, cosine, sine):
    half_width = vectors.shape[-1] // 2
    first_half = vectors[..., :half_width]
    second_half = vectors[..., half_width:]
    cosine = cosine[..., None, :]
    sine = sine[..., None, :]
    return jnp.concatenate(
        [first_half * cosine - second_half * sine, second_half * cosine + first_half * sine],
        axis=-1,
    )


def contract_rows(left, right):
    return lax.dot_general(
        left, right, (((0,), (0,)), ((), ())), preferred_element_type=jnp.float32
    )


def contract_cols(left, right):
    return lax.dot_general(
        left, right, (((1,), (1,)), ((), ())), preferred_element_type=jnp.float32
    )


def norm_backward(grad_normed, source, inv_root, gain_row):
    gain_grad = jnp.sum(grad_normed * source * inv_root, axis=0)
    weighted = grad_normed * gain_row
    back = inv_root * (
        weighted
        - source * inv_root * inv_root * jnp.mean(weighted * source, axis=-1, keepdims=True)
    )
    return (gain_grad, back)


def group_of(kind):
    ctx_at = lax.axis_index("ctx")
    if kind == "wa":
        return lax.axis_size("wa"), lax.axis_index("wa"), lambda p: {"wa": p}
    core = lax.rem(ctx_at, 2)
    if kind == "core":
        return 2, core, lambda p: {"ctx": ctx_at - core + p}
    return lax.axis_size("ctx") // 2, lax.div(ctx_at, 2), lambda p: {"ctx": 2 * p + core}


def exchange_kernel(kind, gather, x_ref, out_ref, own_sem, send_sem, recv_sem):
    count, me, device = group_of(kind)
    own = pltpu.make_async_copy(x_ref if gather else x_ref.at[me], out_ref.at[me], own_sem)
    own.start()
    barrier = pltpu.get_barrier_semaphore()
    for step in range(1, count):
        pl.semaphore_signal(
            barrier,
            inc=1,
            device_id=device(lax.rem(me + step, count)),
            device_id_type=pl.DeviceIdType.MESH,
        )
    pl.semaphore_wait(barrier, count - 1)
    copies = []
    for step in range(1, count):
        peer = lax.rem(me + step, count)
        copy = pltpu.make_async_remote_copy(
            src_ref=x_ref if gather else x_ref.at[peer],
            dst_ref=out_ref.at[me],
            send_sem=send_sem.at[step - 1],
            recv_sem=recv_sem.at[step - 1],
            device_id=device(peer),
            device_id_type=pl.DeviceIdType.MESH,
        )
        copy.start()
        copies.append(copy)
    own.wait()
    for copy in copies:
        copy.wait()


class Links:
    def __init__(self):
        self.ids = {}

    def run(self, kind, gather, x):
        count = group_of(kind)[0]
        out_shape = (count,) + x.shape if gather else x.shape
        key = (kind, gather, x.shape)
        collective = self.ids.setdefault(key, len(self.ids))
        return pl.pallas_call(
            functools.partial(exchange_kernel, kind, gather),
            out_shape=jax.ShapeDtypeStruct(out_shape, x.dtype),
            in_specs=[pl.BlockSpec(memory_space=pl.ANY)],
            out_specs=pl.BlockSpec(memory_space=pl.ANY),
            scratch_shapes=[
                pltpu.SemaphoreType.DMA,
                pltpu.SemaphoreType.DMA((count - 1,)),
                pltpu.SemaphoreType.DMA((count - 1,)),
            ],
            compiler_params=pltpu.CompilerParams(
                collective_id=collective, has_side_effects=True
            ),
        )(x)

    def gather(self, kind, x):
        return self.run(kind, True, x)

    def reduce(self, kind, x):
        return jnp.sum(self.run(kind, False, x.astype(jnp.bfloat16)).astype(jnp.float32), axis=0)


def dot_of(left, right, left_dim, right_dim):
    return lax.dot_general(
        left,
        right,
        (((left_dim,), (right_dim,)), ((), ())),
        preferred_element_type=jnp.float32,
    )


def attend_forward_kernel(q_ref, kv_ref, kpos_ref, qpos_ref, out_ref, lse_ref):
    key_count = kv_ref.shape[0]
    value_at = KEY_VALUE_HEADS * HEAD_SIZE
    query_count = q_ref.shape[1]
    query_pos = qpos_ref[...]
    for head in range(KEY_VALUE_HEADS):
        lo = head * HEAD_SIZE
        query = q_ref[head]

        def body(step, carry):
            top, total, acc = carry
            rows = pl.ds(pl.multiple_of(step * KEY_CHUNK, KEY_CHUNK), KEY_CHUNK)
            key = kv_ref[rows, lo : lo + HEAD_SIZE]
            value = kv_ref[rows, value_at + lo : value_at + lo + HEAD_SIZE]
            live = kpos_ref[rows, :] <= query_pos
            score = jnp.where(live, dot_of(key, query, 1, 1), -1e30)
            new_top = jnp.maximum(top, jnp.max(score, axis=0, keepdims=True))
            prob = jnp.exp(score - new_top)
            keep = jnp.exp(top - new_top)
            total = total * keep + jnp.sum(prob, axis=0, keepdims=True)
            acc = acc * keep + dot_of(value, prob.astype(jnp.bfloat16), 0, 0)
            return new_top, total, acc

        top, total, acc = lax.fori_loop(
            0,
            key_count // KEY_CHUNK,
            body,
            (
                jnp.full((1, query_count), -1e30, jnp.float32),
                jnp.zeros((1, query_count), jnp.float32),
                jnp.zeros((HEAD_SIZE, query_count), jnp.float32),
            ),
        )
        out_ref[head] = acc / total
        lse_ref[head] = top + jnp.log(total)


def attend_backward_kernel(
    q_ref, do_ref, kv_ref, kpos_ref, qpos_ref, lse_ref, delta_ref, dq_ref, dkv_ref
):
    key_count = kv_ref.shape[0]
    value_at = KEY_VALUE_HEADS * HEAD_SIZE
    query_count = q_ref.shape[1]
    query_pos = qpos_ref[...]
    for head in range(KEY_VALUE_HEADS):
        lo = head * HEAD_SIZE
        query = q_ref[head]
        grad = do_ref[head]
        lse = lse_ref[head]
        delta = delta_ref[head]

        def body(step, dquery):
            rows = pl.ds(pl.multiple_of(step * KEY_CHUNK, KEY_CHUNK), KEY_CHUNK)
            key = kv_ref[rows, lo : lo + HEAD_SIZE]
            value = kv_ref[rows, value_at + lo : value_at + lo + HEAD_SIZE]
            live = kpos_ref[rows, :] <= query_pos
            score = jnp.where(live, dot_of(key, query, 1, 1), -1e30)
            prob = jnp.exp(score - lse)
            dscore = (prob * (dot_of(value, grad, 1, 1) - delta)).astype(jnp.bfloat16)
            dkv_ref[rows, lo : lo + HEAD_SIZE] = dot_of(dscore, query, 1, 0).astype(jnp.bfloat16)
            dkv_ref[rows, value_at + lo : value_at + lo + HEAD_SIZE] = dot_of(
                prob.astype(jnp.bfloat16), grad, 1, 0
            ).astype(jnp.bfloat16)
            return dquery + dot_of(key, dscore, 0, 0)

        dq_ref[head] = lax.fori_loop(
            0,
            key_count // KEY_CHUNK,
            body,
            jnp.zeros((HEAD_SIZE, query_count), jnp.float32),
        )


def local_call(kernel, out_shapes, *arrays):
    vmem = pl.BlockSpec(memory_space=pltpu.VMEM)
    return pl.pallas_call(
        kernel,
        out_shape=[jax.ShapeDtypeStruct(s, t) for s, t in out_shapes],
        in_specs=[vmem] * len(arrays),
        out_specs=[vmem] * len(out_shapes),
        compiler_params=pltpu.CompilerParams(vmem_limit_bytes=VMEM_BYTES),
    )(*arrays)


def heads_in(rows):
    count = rows.shape[0]
    split = rows.reshape(count, QUERY_HEADS, HEAD_SIZE).transpose(1, 0, 2)
    return split.reshape(KEY_VALUE_HEADS, -1, HEAD_SIZE)


def heads_out(columns, count):
    split = columns.reshape(KEY_VALUE_HEADS, HEAD_SIZE, -1, count)
    return split.transpose(3, 0, 2, 1).reshape(count, QUERY_HEADS * HEAD_SIZE)


def per_device(
    hidden_in,
    pair_table,
    norm1_gain,
    qkv_weight,
    out_weight,
    norm2_gain,
    gate_up_weight,
    down_weight,
    out_grad,
):
    ctx_count = lax.axis_size("ctx")
    wa_count = lax.axis_size("wa")
    ctx_at = lax.axis_index("ctx")
    wa_at = lax.axis_index("wa")
    links = Links()
    row_count, width = hidden_in.shape
    pairs_total = pair_table.shape[0]
    own_rows = row_count // wa_count
    kv_width = KEY_VALUE_HEADS * HEAD_SIZE
    score_scale = HEAD_SIZE ** (-0.5)
    key_count = ctx_count * row_count
    z_count = ctx_count // 2
    low = jnp.bfloat16
    full = jnp.float32
    seq_blocks = jnp.stack([pair_table, 2 * pairs_total - 1 - pair_table], axis=1).reshape(-1)
    all_pos = (seq_blocks[:, None] * BLK + jnp.arange(BLK, dtype=jnp.int32)[None, :]).reshape(-1)
    own_pos = lax.dynamic_slice_in_dim(
        all_pos, ctx_at * row_count + wa_at * own_rows, own_rows, 0
    )
    query_pos = jnp.tile(own_pos, QUERY_HEADS // KEY_VALUE_HEADS)[None, :]
    key_pos = all_pos.reshape(z_count, 2, wa_count, own_rows).transpose(1, 2, 0, 3).reshape(-1, 1)
    cosine, sine = rotation(own_pos, HEAD_SIZE)

    def own(rows):
        return lax.dynamic_slice_in_dim(rows, wa_at * own_rows, own_rows, 0)

    def gather_rows(rows):
        return links.gather("wa", rows.astype(low)).reshape(row_count, width)

    def reduce_rows(partial_value):
        return links.reduce("wa", partial_value.reshape(wa_count, own_rows, width))

    def rope(rows, heads, sine_of):
        return apply_rotary(rows.reshape(own_rows, heads, HEAD_SIZE), cosine, sine_of).reshape(
            own_rows, heads * HEAD_SIZE
        )

    qkv_full = [links.gather("wa", qkv_weight[0]).reshape(width, -1)]
    qkv_full += [
        lax.all_gather(qkv_weight[layer], "wa", axis=0, tiled=True) for layer in range(1, LAYERS)
    ]
    out_full = [lax.all_gather(out_weight[layer], "wa", axis=0, tiled=True) for layer in range(LAYERS)]
    residual = own(hidden_in).astype(full)
    stored = []
    for layer in range(LAYERS):
        gain_one = norm1_gain[layer].astype(full)
        inv_one = lax.rsqrt(jnp.mean(residual * residual, axis=-1, keepdims=True) + EPSILON)
        normed = (residual * inv_one * gain_one).astype(low)
        qkv = jnp.dot(normed, qkv_full[layer], preferred_element_type=full)
        query = heads_in((rope(qkv[:, :width], QUERY_HEADS, sine).astype(low) * score_scale).astype(low))
        key_value = jnp.concatenate(
            [
                rope(qkv[:, width : width + kv_width], KEY_VALUE_HEADS, sine).astype(low),
                qkv[:, width + kv_width :].astype(low),
            ],
            axis=1,
        )
        key_value = links.gather("z", key_value).reshape(-1, 2 * kv_width)
        key_value = links.gather("wa", key_value).reshape(-1, 2 * kv_width)
        key_value = links.gather("core", key_value).reshape(key_count, 2 * kv_width)
        columns = query.shape[1]
        attended, log_total = local_call(
            attend_forward_kernel,
            [
                ((KEY_VALUE_HEADS, HEAD_SIZE, columns), full),
                ((KEY_VALUE_HEADS, 1, columns), full),
            ],
            query,
            key_value,
            key_pos,
            query_pos,
        )
        weighted = heads_out(attended, own_rows)
        att = weighted.astype(low)
        middle = residual + jnp.dot(att, out_full[layer], preferred_element_type=full)
        gain_two = norm2_gain[layer].astype(full)
        inv_two = lax.rsqrt(jnp.mean(middle * middle, axis=-1, keepdims=True) + EPSILON)
        normed_two = gather_rows((middle * inv_two * gain_two).astype(low))
        gate = jnp.dot(normed_two, gate_up_weight[layer, 0], preferred_element_type=full)
        up = jnp.dot(normed_two, gate_up_weight[layer, 1], preferred_element_type=full)
        activated = (jax.nn.silu(gate) * up).astype(low)
        output_rows = middle + reduce_rows(
            jnp.dot(activated, down_weight[layer], preferred_element_type=full)
        )
        stored.append(
            (residual, inv_one, gain_one, normed, query, key_value, log_total, weighted, att)
            + (middle, inv_two, gain_two, normed_two, gate, up, activated)
        )
        residual = output_rows
    hidden_out = gather_rows(residual).astype(full)
    gradient = own(out_grad).astype(full)
    grad_low = out_grad
    row_grads = [None] * LAYERS
    gate_up_grads = [None] * LAYERS
    down_grads = [None] * LAYERS
    for layer in reversed(range(LAYERS)):
        (
            (layer_input, inv_one, gain_one, normed, query, key_value, log_total, weighted, att)
        ) = stored[layer][:9]
        middle, inv_two, gain_two, normed_two, gate, up, activated = stored[layer][9:]
        down_grads[layer] = contract_rows(activated, grad_low)
        dact = contract_cols(grad_low, down_weight[layer])
        sig = jax.nn.sigmoid(gate)
        dgate = (dact * up * sig * (1.0 + gate * (1.0 - sig))).astype(low)
        dup = (dact * gate * sig).astype(low)
        gate_up_grads[layer] = jnp.stack(
            [contract_rows(normed_two, dgate), contract_rows(normed_two, dup)]
        )
        dnormed_two = reduce_rows(
            contract_cols(dgate, gate_up_weight[layer, 0])
            + contract_cols(dup, gate_up_weight[layer, 1])
        )
        gain_two_grad, dmiddle = norm_backward(dnormed_two, middle, inv_two, gain_two)
        grad_mid = gradient + dmiddle
        mid_low = grad_mid.astype(low)
        out_part = contract_rows(att, mid_low)
        datt = contract_cols(mid_low, out_full[layer]).astype(low)
        delta = jnp.sum(
            (datt.astype(full) * weighted).reshape(own_rows, QUERY_HEADS, HEAD_SIZE), axis=-1
        )
        delta = delta.T.reshape(KEY_VALUE_HEADS, 1, -1)
        columns = query.shape[1]
        dquery, dkv = local_call(
            attend_backward_kernel,
            [
                ((KEY_VALUE_HEADS, HEAD_SIZE, columns), full),
                ((key_count, 2 * kv_width), low),
            ],
            query,
            heads_in(datt),
            key_value,
            key_pos,
            query_pos,
            log_total,
            delta,
        )
        dkv = links.reduce("core", dkv.reshape(2, -1, 2 * kv_width))
        dkv = links.reduce("wa", dkv.reshape(wa_count, -1, 2 * kv_width))
        dkv = links.reduce("z", dkv.reshape(z_count, -1, 2 * kv_width))
        dqkv = jnp.concatenate(
            [
                rope(heads_out(dquery, own_rows) * score_scale, QUERY_HEADS, -sine),
                rope(dkv[:, :kv_width], KEY_VALUE_HEADS, -sine),
                dkv[:, kv_width:],
            ],
            axis=-1,
        ).astype(low)
        qkv_part = contract_rows(normed, dqkv)
        dnormed = contract_cols(dqkv, qkv_full[layer])
        gain_one_grad, dinput = norm_backward(dnormed, layer_input, inv_one, gain_one)
        gradient = grad_mid + dinput
        if layer > 0:
            grad_low = gather_rows(gradient)
        block = jnp.concatenate([qkv_part, out_part], axis=1).astype(low)
        block = block.reshape(wa_count, -1, block.shape[1])
        gains = jnp.concatenate(
            [gain_one_grad, gain_two_grad, jnp.zeros((block.shape[2] - 2 * width,), full)]
        ).astype(low)
        pad_rows = 16 + (-block.shape[1]) % 16
        gains = jnp.broadcast_to(gains, (wa_count, pad_rows, gains.shape[0]))
        row_grads[layer] = links.reduce("wa", jnp.concatenate([block, gains], axis=1))
    input_grad = gather_rows(gradient).astype(full)
    slab = qkv_weight.shape[1]
    rows_sum, gate_up_sum, down_sum = (
        lax.psum(jnp.stack(part).astype(low), "ctx").astype(full)
        for part in (row_grads, gate_up_grads, down_grads)
    )
    qkv_cols = qkv_weight.shape[2]
    return (
        hidden_out,
        input_grad,
        rows_sum[:, slab, :width],
        rows_sum[:, :slab, :qkv_cols],
        rows_sum[:, :slab, qkv_cols:],
        rows_sum[:, slab, width : 2 * width],
        gate_up_sum,
        down_sum,
    )


def solution(mesh):
    placed = (
        P("ctx", None),
        P(),
        P(),
        P(None, "wa", None),
        P(None, "wa", None),
        P(),
        P(None, None, None, "wa"),
        P(None, "wa", None),
        P("ctx", None),
    )
    return jax.shard_map(
        per_device,
        mesh=mesh,
        in_specs=placed,
        out_specs=(
            P("ctx", None),
            P("ctx", None),
            P(),
            P(None, "wa", None),
            P(None, "wa", None),
            P(),
            P(None, None, None, "wa"),
            P(None, "wa", None),
        ),
        check_vma=False,
    )
```

```python
import functools

import jax
import jax.numpy as jnp
from jax import lax
from jax.experimental import pallas as pl
from jax.experimental.pallas import tpu as pltpu
from jax.sharding import PartitionSpec as P

QUERY_HEADS = 9
KEY_VALUE_HEADS = 3
HEAD_SIZE = 64
BLK = 128
LAYERS = 2


EPSILON = 1e-05
KEY_CHUNK = 512
VMEM_BYTES = 50 * 1024 * 1024
LINK_VMEM_BYTES = 24 * 1024 * 1024


def rotation(token_pos, head_width):
    half_width = head_width // 2
    inv_freq = jnp.power(
        jnp.float32(100000.0), -2.0 * jnp.arange(half_width, dtype=jnp.float32) / head_width
    )
    angles = token_pos.astype(jnp.float32)[..., None] * inv_freq
    return (jnp.cos(angles), jnp.sin(angles))


def apply_rotary(vectors, cosine, sine):
    half_width = vectors.shape[-1] // 2
    first_half = vectors[..., :half_width]
    second_half = vectors[..., half_width:]
    cosine = cosine[..., None, :]
    sine = sine[..., None, :]
    return jnp.concatenate(
        [first_half * cosine - second_half * sine, second_half * cosine + first_half * sine],
        axis=-1,
    )


def contract_rows(left, right):
    return lax.dot_general(
        left, right, (((0,), (0,)), ((), ())), preferred_element_type=jnp.float32
    )


def contract_cols(left, right):
    return lax.dot_general(
        left, right, (((1,), (1,)), ((), ())), preferred_element_type=jnp.float32
    )


def norm_backward(grad_normed, source, inv_root, gain_row):
    gain_grad = jnp.sum(grad_normed * source * inv_root, axis=0)
    weighted = grad_normed * gain_row
    back = inv_root * (
        weighted
        - source * inv_root * inv_root * jnp.mean(weighted * source, axis=-1, keepdims=True)
    )
    return (gain_grad, back)


def group_of(kind):
    ctx_at = lax.axis_index("ctx")
    if kind == "wa":
        return lax.axis_size("wa"), lax.axis_index("wa"), lambda p: {"wa": p}
    if kind == "ctx":
        return lax.axis_size("ctx"), ctx_at, lambda p: {"ctx": p}
    core = lax.rem(ctx_at, 2)
    if kind == "core":
        return 2, core, lambda p: {"ctx": ctx_at - core + p}
    return lax.axis_size("ctx") // 2, lax.div(ctx_at, 2), lambda p: {"ctx": 2 * p + core}


def exchange_kernel(kind, gather, x_ref, out_ref, own_sem, send_sem, recv_sem):
    count, me, device = group_of(kind)
    own = pltpu.make_async_copy(x_ref if gather else x_ref.at[me], out_ref.at[me], own_sem)
    own.start()
    barrier = pltpu.get_barrier_semaphore()
    for step in range(1, count):
        pl.semaphore_signal(
            barrier,
            inc=1,
            device_id=device(lax.rem(me + step, count)),
            device_id_type=pl.DeviceIdType.MESH,
        )
    pl.semaphore_wait(barrier, count - 1)
    copies = []
    for step in range(1, count):
        peer = lax.rem(me + step, count)
        copy = pltpu.make_async_remote_copy(
            src_ref=x_ref if gather else x_ref.at[peer],
            dst_ref=out_ref.at[me],
            send_sem=send_sem.at[step - 1],
            recv_sem=recv_sem.at[step - 1],
            device_id=device(peer),
            device_id_type=pl.DeviceIdType.MESH,
        )
        copy.start()
        copies.append(copy)
    own.wait()
    for copy in copies:
        copy.wait()


class Links:
    def __init__(self):
        self.ids = {}

    def run(self, kind, gather, x):
        count = group_of(kind)[0]
        out_shape = (count,) + x.shape if gather else x.shape
        key = (kind, gather, x.shape)
        collective = self.ids.setdefault(key, len(self.ids))
        return pl.pallas_call(
            functools.partial(exchange_kernel, kind, gather),
            out_shape=jax.ShapeDtypeStruct(out_shape, x.dtype),
            in_specs=[pl.BlockSpec(memory_space=pltpu.VMEM)],
            out_specs=pl.BlockSpec(memory_space=pltpu.VMEM),
            scratch_shapes=[
                pltpu.SemaphoreType.DMA,
                pltpu.SemaphoreType.DMA((count - 1,)),
                pltpu.SemaphoreType.DMA((count - 1,)),
            ],
            compiler_params=pltpu.CompilerParams(
                collective_id=collective,
                has_side_effects=True,
                vmem_limit_bytes=LINK_VMEM_BYTES,
            ),
        )(x)

    def gather(self, kind, x):
        return self.run(kind, True, x)

    def reduce(self, kind, x):
        return jnp.sum(self.run(kind, False, x.astype(jnp.bfloat16)).astype(jnp.float32), axis=0)


def sum_over_ctx(links, x):
    count = lax.axis_size("ctx")
    high, wide = x.shape
    tiles = x.reshape(high // 16, 16, wide // 128, 128).transpose(0, 2, 1, 3).reshape(-1, 16, 128)
    number = tiles.shape[0]
    tiles = jnp.pad(tiles.astype(jnp.bfloat16), ((0, -number % count), (0, 0), (0, 0)))
    part = links.reduce("ctx", tiles.reshape(count, -1, 128))
    total = links.gather("ctx", part.astype(jnp.bfloat16)).reshape(-1, 16, 128)[:number]
    total = total.reshape(high // 16, wide // 128, 16, 128).transpose(0, 2, 1, 3)
    return total.reshape(high, wide)


def dot_of(left, right, left_dim, right_dim):
    return lax.dot_general(
        left,
        right,
        (((left_dim,), (right_dim,)), ((), ())),
        preferred_element_type=jnp.float32,
    )


def attend_forward_kernel(q_ref, kv_ref, kpos_ref, qpos_ref, out_ref, lse_ref):
    key_count = kv_ref.shape[0]
    value_at = KEY_VALUE_HEADS * HEAD_SIZE
    query_count = q_ref.shape[1]
    query_pos = qpos_ref[...]
    for head in range(KEY_VALUE_HEADS):
        lo = head * HEAD_SIZE
        query = q_ref[head]

        def body(step, carry):
            top, total, acc = carry
            rows = pl.ds(pl.multiple_of(step * KEY_CHUNK, KEY_CHUNK), KEY_CHUNK)
            key = kv_ref[rows, lo : lo + HEAD_SIZE]
            value = kv_ref[rows, value_at + lo : value_at + lo + HEAD_SIZE]
            live = kpos_ref[rows, :] <= query_pos
            score = jnp.where(live, dot_of(key, query, 1, 1), -1e30)
            new_top = jnp.maximum(top, jnp.max(score, axis=0, keepdims=True))
            prob = jnp.exp(score - new_top)
            keep = jnp.exp(top - new_top)
            total = total * keep + jnp.sum(prob, axis=0, keepdims=True)
            acc = acc * keep + dot_of(value, prob.astype(jnp.bfloat16), 0, 0)
            return new_top, total, acc

        top, total, acc = lax.fori_loop(
            0,
            key_count // KEY_CHUNK,
            body,
            (
                jnp.full((1, query_count), -1e30, jnp.float32),
                jnp.zeros((1, query_count), jnp.float32),
                jnp.zeros((HEAD_SIZE, query_count), jnp.float32),
            ),
        )
        out_ref[head] = acc / total
        lse_ref[head] = top + jnp.log(total)


def attend_backward_kernel(
    q_ref, do_ref, kv_ref, kpos_ref, qpos_ref, lse_ref, delta_ref, dq_ref, dkv_ref
):
    key_count = kv_ref.shape[0]
    value_at = KEY_VALUE_HEADS * HEAD_SIZE
    query_count = q_ref.shape[1]
    query_pos = qpos_ref[...]
    for head in range(KEY_VALUE_HEADS):
        lo = head * HEAD_SIZE
        query = q_ref[head]
        grad = do_ref[head]
        lse = lse_ref[head]
        delta = delta_ref[head]

        def body(step, dquery):
            rows = pl.ds(pl.multiple_of(step * KEY_CHUNK, KEY_CHUNK), KEY_CHUNK)
            key = kv_ref[rows, lo : lo + HEAD_SIZE]
            value = kv_ref[rows, value_at + lo : value_at + lo + HEAD_SIZE]
            live = kpos_ref[rows, :] <= query_pos
            score = jnp.where(live, dot_of(key, query, 1, 1), -1e30)
            prob = jnp.exp(score - lse)
            dscore = (prob * (dot_of(value, grad, 1, 1) - delta)).astype(jnp.bfloat16)
            dkv_ref[rows, lo : lo + HEAD_SIZE] = dot_of(dscore, query, 1, 0).astype(jnp.bfloat16)
            dkv_ref[rows, value_at + lo : value_at + lo + HEAD_SIZE] = dot_of(
                prob.astype(jnp.bfloat16), grad, 1, 0
            ).astype(jnp.bfloat16)
            return dquery + dot_of(key, dscore, 0, 0)

        dq_ref[head] = lax.fori_loop(
            0,
            key_count // KEY_CHUNK,
            body,
            jnp.zeros((HEAD_SIZE, query_count), jnp.float32),
        )


def local_call(kernel, out_shapes, *arrays):
    vmem = pl.BlockSpec(memory_space=pltpu.VMEM)
    return pl.pallas_call(
        kernel,
        out_shape=[jax.ShapeDtypeStruct(s, t) for s, t in out_shapes],
        in_specs=[vmem] * len(arrays),
        out_specs=[vmem] * len(out_shapes),
        compiler_params=pltpu.CompilerParams(vmem_limit_bytes=VMEM_BYTES),
    )(*arrays)


def heads_in(rows):
    count = rows.shape[0]
    split = rows.reshape(count, QUERY_HEADS, HEAD_SIZE).transpose(1, 0, 2)
    return split.reshape(KEY_VALUE_HEADS, -1, HEAD_SIZE)


def heads_out(columns, count):
    split = columns.reshape(KEY_VALUE_HEADS, HEAD_SIZE, -1, count)
    return split.transpose(3, 0, 2, 1).reshape(count, QUERY_HEADS * HEAD_SIZE)


def per_device(
    hidden_in,
    pair_table,
    norm1_gain,
    qkv_weight,
    out_weight,
    norm2_gain,
    gate_up_weight,
    down_weight,
    out_grad,
):
    ctx_count = lax.axis_size("ctx")
    wa_count = lax.axis_size("wa")
    ctx_at = lax.axis_index("ctx")
    wa_at = lax.axis_index("wa")
    links = Links()
    row_count, width = hidden_in.shape
    pairs_total = pair_table.shape[0]
    own_rows = row_count // wa_count
    kv_width = KEY_VALUE_HEADS * HEAD_SIZE
    score_scale = HEAD_SIZE ** (-0.5)
    key_count = ctx_count * row_count
    z_count = ctx_count // 2
    low = jnp.bfloat16
    full = jnp.float32
    seq_blocks = jnp.stack([pair_table, 2 * pairs_total - 1 - pair_table], axis=1).reshape(-1)
    all_pos = (seq_blocks[:, None] * BLK + jnp.arange(BLK, dtype=jnp.int32)[None, :]).reshape(-1)
    own_pos = lax.dynamic_slice_in_dim(
        all_pos, ctx_at * row_count + wa_at * own_rows, own_rows, 0
    )
    query_pos = jnp.tile(own_pos, QUERY_HEADS // KEY_VALUE_HEADS)[None, :]
    key_pos = all_pos.reshape(z_count, 2, wa_count, own_rows).transpose(1, 2, 0, 3).reshape(-1, 1)
    cosine, sine = rotation(own_pos, HEAD_SIZE)

    def own(rows):
        return lax.dynamic_slice_in_dim(rows, wa_at * own_rows, own_rows, 0)

    def gather_rows(rows):
        return links.gather("wa", rows.astype(low)).reshape(row_count, width)

    def reduce_rows(partial_value):
        return links.reduce("wa", partial_value.reshape(wa_count, own_rows, width))

    def rope(rows, heads, sine_of):
        return apply_rotary(rows.reshape(own_rows, heads, HEAD_SIZE), cosine, sine_of).reshape(
            own_rows, heads * HEAD_SIZE
        )

    qkv_cols = qkv_weight.shape[2]
    slab = qkv_weight.shape[1]
    later = jnp.concatenate([out_weight[0], out_weight[1], qkv_weight[1]], axis=1)
    later = lax.all_gather(later, "wa", axis=0, tiled=True)
    out_full = [later[:, :width], later[:, width : 2 * width]]
    qkv_full = [links.gather("wa", qkv_weight[0]).reshape(width, -1), later[:, 2 * width :]]
    residual = own(hidden_in).astype(full)
    stored = []
    for layer in range(LAYERS):
        gain_one = norm1_gain[layer].astype(full)
        inv_one = lax.rsqrt(jnp.mean(residual * residual, axis=-1, keepdims=True) + EPSILON)
        normed = (residual * inv_one * gain_one).astype(low)
        qkv = jnp.dot(normed, qkv_full[layer], preferred_element_type=full)
        query = heads_in((rope(qkv[:, :width], QUERY_HEADS, sine).astype(low) * score_scale).astype(low))
        key_value = jnp.concatenate(
            [
                rope(qkv[:, width : width + kv_width], KEY_VALUE_HEADS, sine).astype(low),
                qkv[:, width + kv_width :].astype(low),
            ],
            axis=1,
        )
        key_value = links.gather("z", key_value).reshape(-1, 2 * kv_width)
        key_value = links.gather("wa", key_value).reshape(-1, 2 * kv_width)
        key_value = links.gather("core", key_value).reshape(key_count, 2 * kv_width)
        columns = query.shape[1]
        attended, log_total = local_call(
            attend_forward_kernel,
            [
                ((KEY_VALUE_HEADS, HEAD_SIZE, columns), full),
                ((KEY_VALUE_HEADS, 1, columns), full),
            ],
            query,
            key_value,
            key_pos,
            query_pos,
        )
        weighted = heads_out(attended, own_rows)
        att = weighted.astype(low)
        middle = residual + jnp.dot(att, out_full[layer], preferred_element_type=full)
        gain_two = norm2_gain[layer].astype(full)
        inv_two = lax.rsqrt(jnp.mean(middle * middle, axis=-1, keepdims=True) + EPSILON)
        normed_two = gather_rows((middle * inv_two * gain_two).astype(low))
        gate = jnp.dot(normed_two, gate_up_weight[layer, 0], preferred_element_type=full)
        up = jnp.dot(normed_two, gate_up_weight[layer, 1], preferred_element_type=full)
        activated = (jax.nn.silu(gate) * up).astype(low)
        output_rows = middle + reduce_rows(
            jnp.dot(activated, down_weight[layer], preferred_element_type=full)
        )
        stored.append(
            (residual, inv_one, gain_one, normed, query, key_value, log_total, weighted, att)
            + (middle, inv_two, gain_two, normed_two, gate, up, activated)
        )
        residual = output_rows
    hidden_own = residual.astype(low)
    gradient = own(out_grad).astype(full)
    grad_low = out_grad
    row_grads = [None] * LAYERS
    gate_up_grads = [None] * LAYERS
    down_grads = [None] * LAYERS
    for layer in reversed(range(LAYERS)):
        (
            (layer_input, inv_one, gain_one, normed, query, key_value, log_total, weighted, att)
        ) = stored[layer][:9]
        middle, inv_two, gain_two, normed_two, gate, up, activated = stored[layer][9:]
        down_grads[layer] = contract_rows(activated, grad_low)
        dact = contract_cols(grad_low, down_weight[layer])
        sig = jax.nn.sigmoid(gate)
        dgate = (dact * up * sig * (1.0 + gate * (1.0 - sig))).astype(low)
        dup = (dact * gate * sig).astype(low)
        gate_up_grads[layer] = jnp.stack(
            [contract_rows(normed_two, dgate), contract_rows(normed_two, dup)]
        )
        dnormed_two = reduce_rows(
            contract_cols(dgate, gate_up_weight[layer, 0])
            + contract_cols(dup, gate_up_weight[layer, 1])
        )
        if layer == 0:
            early = (row_grads[1].astype(low), jnp.stack(gate_up_grads).astype(low))
            early = lax.psum(early + (jnp.stack(down_grads).astype(low),), "ctx")
        gain_two_grad, dmiddle = norm_backward(dnormed_two, middle, inv_two, gain_two)
        grad_mid = gradient + dmiddle
        mid_low = grad_mid.astype(low)
        out_part = contract_rows(att, mid_low)
        datt = contract_cols(mid_low, out_full[layer]).astype(low)
        delta = jnp.sum(
            (datt.astype(full) * weighted).reshape(own_rows, QUERY_HEADS, HEAD_SIZE), axis=-1
        )
        delta = delta.T.reshape(KEY_VALUE_HEADS, 1, -1)
        columns = query.shape[1]
        dquery, dkv = local_call(
            attend_backward_kernel,
            [
                ((KEY_VALUE_HEADS, HEAD_SIZE, columns), full),
                ((key_count, 2 * kv_width), low),
            ],
            query,
            heads_in(datt),
            key_value,
            key_pos,
            query_pos,
            log_total,
            delta,
        )
        dkv = links.reduce("core", dkv.reshape(2, -1, 2 * kv_width))
        dkv = links.reduce("wa", dkv.reshape(wa_count, -1, 2 * kv_width))
        dkv = links.reduce("z", dkv.reshape(z_count, -1, 2 * kv_width))
        dqkv = jnp.concatenate(
            [
                rope(heads_out(dquery, own_rows) * score_scale, QUERY_HEADS, -sine),
                rope(dkv[:, :kv_width], KEY_VALUE_HEADS, -sine),
                dkv[:, kv_width:],
            ],
            axis=-1,
        ).astype(low)
        qkv_part = contract_rows(normed, dqkv)
        dnormed = contract_cols(dqkv, qkv_full[layer])
        gain_one_grad, dinput = norm_backward(dnormed, layer_input, inv_one, gain_one)
        gradient = grad_mid + dinput
        if layer > 0:
            grad_low = gather_rows(gradient)
        block = jnp.concatenate([qkv_part, out_part], axis=1).astype(low)
        block = block.reshape(wa_count, -1, block.shape[1])
        gains = jnp.concatenate(
            [gain_one_grad, gain_two_grad, jnp.zeros((block.shape[2] - 2 * width,), full)]
        ).astype(low)
        pad_rows = 16 + (-block.shape[1]) % 16
        gains = jnp.broadcast_to(gains, (wa_count, pad_rows, gains.shape[0]))
        row_grads[layer] = links.reduce("wa", jnp.concatenate([block, gains], axis=1))
        if layer > 0:
            grad_low, row_grads[layer] = lax.optimization_barrier((grad_low, row_grads[layer]))
    ends = links.gather("wa", jnp.stack([hidden_own, gradient.astype(low)])).astype(full)
    hidden_out, input_grad = (ends[:, at].reshape(row_count, width) for at in range(2))
    rows_sum = jnp.stack([sum_over_ctx(links, row_grads[0]), early[0]]).astype(full)
    gate_up_sum = early[1].astype(full)
    down_sum = early[2].astype(full)
    return (
        hidden_out,
        input_grad,
        rows_sum[:, slab, :width],
        rows_sum[:, :slab, :qkv_cols],
        rows_sum[:, :slab, qkv_cols:],
        rows_sum[:, slab, width : 2 * width],
        gate_up_sum,
        down_sum,
    )


def solution(mesh):
    placed = (
        P("ctx", None),
        P(),
        P(),
        P(None, "wa", None),
        P(None, "wa", None),
        P(),
        P(None, None, None, "wa"),
        P(None, "wa", None),
        P("ctx", None),
    )
    return jax.shard_map(
        per_device,
        mesh=mesh,
        in_specs=placed,
        out_specs=(
            P("ctx", None),
            P("ctx", None),
            P(),
            P(None, "wa", None),
            P(None, "wa", None),
            P(),
            P(None, None, None, "wa"),
            P(None, "wa", None),
        ),
        check_vma=False,
    )
```

```python
import functools

import jax
import jax.numpy as jnp
from jax import lax
from jax.experimental import pallas as pl
from jax.experimental.pallas import tpu as pltpu
from jax.sharding import PartitionSpec as P

QUERY_HEADS = 9
KEY_VALUE_HEADS = 3
HEAD_SIZE = 64
BLK = 128
LAYERS = 2


EPSILON = 1e-05
KEY_CHUNK = 1024
VMEM_BYTES = 50 * 1024 * 1024
LINK_VMEM_BYTES = 24 * 1024 * 1024


def rotation(token_pos, head_width):
    half_width = head_width // 2
    inv_freq = jnp.power(
        jnp.float32(100000.0), -2.0 * jnp.arange(half_width, dtype=jnp.float32) / head_width
    )
    angles = token_pos.astype(jnp.float32)[..., None] * inv_freq
    return (jnp.cos(angles), jnp.sin(angles))


def apply_rotary(vectors, cosine, sine):
    half_width = vectors.shape[-1] // 2
    first_half = vectors[..., :half_width]
    second_half = vectors[..., half_width:]
    cosine = cosine[..., None, :]
    sine = sine[..., None, :]
    return jnp.concatenate(
        [first_half * cosine - second_half * sine, second_half * cosine + first_half * sine],
        axis=-1,
    )


def contract_rows(left, right):
    return lax.dot_general(
        left, right, (((0,), (0,)), ((), ())), preferred_element_type=jnp.float32
    )


def contract_cols(left, right):
    return lax.dot_general(
        left, right, (((1,), (1,)), ((), ())), preferred_element_type=jnp.float32
    )


def norm_backward(grad_normed, source, inv_root, gain_row):
    gain_grad = jnp.sum(grad_normed * source * inv_root, axis=0)
    weighted = grad_normed * gain_row
    back = inv_root * (
        weighted
        - source * inv_root * inv_root * jnp.mean(weighted * source, axis=-1, keepdims=True)
    )
    return (gain_grad, back)


def group_of(kind):
    ctx_at = lax.axis_index("ctx")
    if kind == "wa":
        return lax.axis_size("wa"), lax.axis_index("wa"), lambda p: {"wa": p}
    if kind == "ctx":
        return lax.axis_size("ctx"), ctx_at, lambda p: {"ctx": p}
    core = lax.rem(ctx_at, 2)
    if kind == "core":
        return 2, core, lambda p: {"ctx": ctx_at - core + p}
    return lax.axis_size("ctx") // 2, lax.div(ctx_at, 2), lambda p: {"ctx": 2 * p + core}


def exchange_kernel(kind, gather, x_ref, out_ref, own_sem, send_sem, recv_sem):
    count, me, device = group_of(kind)
    own = pltpu.make_async_copy(x_ref if gather else x_ref.at[me], out_ref.at[me], own_sem)
    own.start()
    barrier = pltpu.get_barrier_semaphore()
    for step in range(1, count):
        pl.semaphore_signal(
            barrier,
            inc=1,
            device_id=device(lax.rem(me + step, count)),
            device_id_type=pl.DeviceIdType.MESH,
        )
    pl.semaphore_wait(barrier, count - 1)
    copies = []
    for step in range(1, count):
        peer = lax.rem(me + step, count)
        copy = pltpu.make_async_remote_copy(
            src_ref=x_ref if gather else x_ref.at[peer],
            dst_ref=out_ref.at[me],
            send_sem=send_sem.at[step - 1],
            recv_sem=recv_sem.at[step - 1],
            device_id=device(peer),
            device_id_type=pl.DeviceIdType.MESH,
        )
        copy.start()
        copies.append(copy)
    own.wait()
    for copy in copies:
        copy.wait()


class Links:
    def __init__(self):
        self.ids = {}

    def run(self, kind, gather, x):
        count = group_of(kind)[0]
        out_shape = (count,) + x.shape if gather else x.shape
        key = (kind, gather, x.shape)
        collective = self.ids.setdefault(key, len(self.ids))
        return pl.pallas_call(
            functools.partial(exchange_kernel, kind, gather),
            out_shape=jax.ShapeDtypeStruct(out_shape, x.dtype),
            in_specs=[pl.BlockSpec(memory_space=pltpu.VMEM)],
            out_specs=pl.BlockSpec(memory_space=pltpu.VMEM),
            scratch_shapes=[
                pltpu.SemaphoreType.DMA,
                pltpu.SemaphoreType.DMA((count - 1,)),
                pltpu.SemaphoreType.DMA((count - 1,)),
            ],
            compiler_params=pltpu.CompilerParams(
                collective_id=collective,
                has_side_effects=True,
                vmem_limit_bytes=LINK_VMEM_BYTES,
            ),
        )(x)

    def gather(self, kind, x):
        return self.run(kind, True, x)

    def reduce(self, kind, x):
        return jnp.sum(self.run(kind, False, x.astype(jnp.bfloat16)).astype(jnp.float32), axis=0)


def sum_over_ctx(links, x):
    count = lax.axis_size("ctx")
    high, wide = x.shape
    tiles = x.reshape(high // 16, 16, wide // 128, 128).transpose(0, 2, 1, 3).reshape(-1, 16, 128)
    number = tiles.shape[0]
    tiles = jnp.pad(tiles.astype(jnp.bfloat16), ((0, -number % count), (0, 0), (0, 0)))
    part = links.reduce("ctx", tiles.reshape(count, -1, 128))
    total = links.gather("ctx", part.astype(jnp.bfloat16)).reshape(-1, 16, 128)[:number]
    total = total.reshape(high // 16, wide // 128, 16, 128).transpose(0, 2, 1, 3)
    return total.reshape(high, wide)


def dot_of(left, right, left_dim, right_dim):
    return lax.dot_general(
        left,
        right,
        (((left_dim,), (right_dim,)), ((), ())),
        preferred_element_type=jnp.float32,
    )


def attend_forward_kernel(q_ref, kv_ref, kpos_ref, qpos_ref, out_ref, lse_ref):
    key_count = kv_ref.shape[0]
    value_at = KEY_VALUE_HEADS * HEAD_SIZE
    query_count = q_ref.shape[1]
    query_pos = qpos_ref[...]
    for head in range(KEY_VALUE_HEADS):
        lo = head * HEAD_SIZE
        query = q_ref[head]

        def body(step, carry):
            top, total, acc = carry
            rows = pl.ds(pl.multiple_of(step * KEY_CHUNK, KEY_CHUNK), KEY_CHUNK)
            key = kv_ref[rows, lo : lo + HEAD_SIZE]
            value = kv_ref[rows, value_at + lo : value_at + lo + HEAD_SIZE]
            live = kpos_ref[rows, :] <= query_pos
            score = jnp.where(live, dot_of(key, query, 1, 1), -1e30)
            new_top = jnp.maximum(top, jnp.max(score, axis=0, keepdims=True))
            prob = jnp.exp(score - new_top)
            keep = jnp.exp(top - new_top)
            total = total * keep + jnp.sum(prob, axis=0, keepdims=True)
            acc = acc * keep + dot_of(value, prob.astype(jnp.bfloat16), 0, 0)
            return new_top, total, acc

        top, total, acc = lax.fori_loop(
            0,
            key_count // KEY_CHUNK,
            body,
            (
                jnp.full((1, query_count), -1e30, jnp.float32),
                jnp.zeros((1, query_count), jnp.float32),
                jnp.zeros((HEAD_SIZE, query_count), jnp.float32),
            ),
        )
        out_ref[head] = acc / total
        lse_ref[head] = top + jnp.log(total)


def attend_backward_kernel(
    q_ref, do_ref, kv_ref, kpos_ref, qpos_ref, lse_ref, delta_ref, dq_ref, dkv_ref
):
    key_count = kv_ref.shape[0]
    value_at = KEY_VALUE_HEADS * HEAD_SIZE
    query_count = q_ref.shape[1]
    query_pos = qpos_ref[...]
    for head in range(KEY_VALUE_HEADS):
        lo = head * HEAD_SIZE
        query = q_ref[head]
        grad = do_ref[head]
        lse = lse_ref[head]
        delta = delta_ref[head]

        def body(step, dquery):
            rows = pl.ds(pl.multiple_of(step * KEY_CHUNK, KEY_CHUNK), KEY_CHUNK)
            key = kv_ref[rows, lo : lo + HEAD_SIZE]
            value = kv_ref[rows, value_at + lo : value_at + lo + HEAD_SIZE]
            live = kpos_ref[rows, :] <= query_pos
            score = jnp.where(live, dot_of(key, query, 1, 1), -1e30)
            prob = jnp.exp(score - lse)
            dscore = (prob * (dot_of(value, grad, 1, 1) - delta)).astype(jnp.bfloat16)
            dkv_ref[rows, lo : lo + HEAD_SIZE] = dot_of(dscore, query, 1, 0).astype(jnp.bfloat16)
            dkv_ref[rows, value_at + lo : value_at + lo + HEAD_SIZE] = dot_of(
                prob.astype(jnp.bfloat16), grad, 1, 0
            ).astype(jnp.bfloat16)
            return dquery + dot_of(key, dscore, 0, 0)

        dq_ref[head] = lax.fori_loop(
            0,
            key_count // KEY_CHUNK,
            body,
            jnp.zeros((HEAD_SIZE, query_count), jnp.float32),
        )


def local_call(kernel, out_shapes, *arrays):
    vmem = pl.BlockSpec(memory_space=pltpu.VMEM)
    return pl.pallas_call(
        kernel,
        out_shape=[jax.ShapeDtypeStruct(s, t) for s, t in out_shapes],
        in_specs=[vmem] * len(arrays),
        out_specs=[vmem] * len(out_shapes),
        compiler_params=pltpu.CompilerParams(vmem_limit_bytes=VMEM_BYTES),
    )(*arrays)


def heads_in(rows):
    count = rows.shape[0]
    split = rows.reshape(count, QUERY_HEADS, HEAD_SIZE).transpose(1, 0, 2)
    return split.reshape(KEY_VALUE_HEADS, -1, HEAD_SIZE)


def heads_out(columns, count):
    split = columns.reshape(KEY_VALUE_HEADS, HEAD_SIZE, -1, count)
    return split.transpose(3, 0, 2, 1).reshape(count, QUERY_HEADS * HEAD_SIZE)


def per_device(
    hidden_in,
    pair_table,
    norm1_gain,
    qkv_weight,
    out_weight,
    norm2_gain,
    gate_up_weight,
    down_weight,
    out_grad,
):
    ctx_count = lax.axis_size("ctx")
    wa_count = lax.axis_size("wa")
    ctx_at = lax.axis_index("ctx")
    wa_at = lax.axis_index("wa")
    links = Links()
    row_count, width = hidden_in.shape
    pairs_total = pair_table.shape[0]
    own_rows = row_count // wa_count
    kv_width = KEY_VALUE_HEADS * HEAD_SIZE
    score_scale = HEAD_SIZE ** (-0.5)
    key_count = ctx_count * row_count
    z_count = ctx_count // 2
    low = jnp.bfloat16
    full = jnp.float32
    seq_blocks = jnp.stack([pair_table, 2 * pairs_total - 1 - pair_table], axis=1).reshape(-1)
    all_pos = (seq_blocks[:, None] * BLK + jnp.arange(BLK, dtype=jnp.int32)[None, :]).reshape(-1)
    own_pos = lax.dynamic_slice_in_dim(
        all_pos, ctx_at * row_count + wa_at * own_rows, own_rows, 0
    )
    query_pos = jnp.tile(own_pos, QUERY_HEADS // KEY_VALUE_HEADS)[None, :]
    key_pos = all_pos.reshape(z_count, 2, wa_count, own_rows).transpose(1, 2, 0, 3).reshape(-1, 1)
    cosine, sine = rotation(own_pos, HEAD_SIZE)

    def own(rows):
        return lax.dynamic_slice_in_dim(rows, wa_at * own_rows, own_rows, 0)

    def gather_rows(rows):
        return links.gather("wa", rows.astype(low)).reshape(row_count, width)

    def reduce_rows(partial_value):
        return links.reduce("wa", partial_value.reshape(wa_count, own_rows, width))

    def rope(rows, heads, sine_of):
        return apply_rotary(rows.reshape(own_rows, heads, HEAD_SIZE), cosine, sine_of).reshape(
            own_rows, heads * HEAD_SIZE
        )

    qkv_cols = qkv_weight.shape[2]
    slab = qkv_weight.shape[1]
    later = jnp.concatenate([out_weight[0], out_weight[1], qkv_weight[1]], axis=1)
    later = lax.all_gather(later, "wa", axis=0, tiled=True)
    out_full = [later[:, :width], later[:, width : 2 * width]]
    qkv_full = [links.gather("wa", qkv_weight[0]).reshape(width, -1), later[:, 2 * width :]]
    residual = own(hidden_in).astype(full)
    stored = []
    for layer in range(LAYERS):
        gain_one = norm1_gain[layer].astype(full)
        inv_one = lax.rsqrt(jnp.mean(residual * residual, axis=-1, keepdims=True) + EPSILON)
        normed = (residual * inv_one * gain_one).astype(low)
        qkv = jnp.dot(normed, qkv_full[layer], preferred_element_type=full)
        query = heads_in((rope(qkv[:, :width], QUERY_HEADS, sine).astype(low) * score_scale).astype(low))
        key_value = jnp.concatenate(
            [
                rope(qkv[:, width : width + kv_width], KEY_VALUE_HEADS, sine).astype(low),
                qkv[:, width + kv_width :].astype(low),
            ],
            axis=1,
        )
        key_value = links.gather("z", key_value).reshape(-1, 2 * kv_width)
        key_value = links.gather("wa", key_value).reshape(-1, 2 * kv_width)
        key_value = links.gather("core", key_value).reshape(key_count, 2 * kv_width)
        columns = query.shape[1]
        attended, log_total = local_call(
            attend_forward_kernel,
            [
                ((KEY_VALUE_HEADS, HEAD_SIZE, columns), full),
                ((KEY_VALUE_HEADS, 1, columns), full),
            ],
            query,
            key_value,
            key_pos,
            query_pos,
        )
        weighted = heads_out(attended, own_rows)
        att = weighted.astype(low)
        middle = residual + jnp.dot(att, out_full[layer], preferred_element_type=full)
        gain_two = norm2_gain[layer].astype(full)
        inv_two = lax.rsqrt(jnp.mean(middle * middle, axis=-1, keepdims=True) + EPSILON)
        normed_two = gather_rows((middle * inv_two * gain_two).astype(low))
        gate = jnp.dot(normed_two, gate_up_weight[layer, 0], preferred_element_type=full)
        up = jnp.dot(normed_two, gate_up_weight[layer, 1], preferred_element_type=full)
        activated = (jax.nn.silu(gate) * up).astype(low)
        output_rows = middle + reduce_rows(
            jnp.dot(activated, down_weight[layer], preferred_element_type=full)
        )
        stored.append(
            (residual, inv_one, gain_one, normed, query, key_value, log_total, weighted, att)
            + (middle, inv_two, gain_two, normed_two, gate, up, activated)
        )
        residual = output_rows
    hidden_own = residual.astype(low)
    gradient = own(out_grad).astype(full)
    grad_low = out_grad
    row_grads = [None] * LAYERS
    gate_up_grads = [None] * LAYERS
    down_grads = [None] * LAYERS
    for layer in reversed(range(LAYERS)):
        (
            (layer_input, inv_one, gain_one, normed, query, key_value, log_total, weighted, att)
        ) = stored[layer][:9]
        middle, inv_two, gain_two, normed_two, gate, up, activated = stored[layer][9:]
        down_grads[layer] = contract_rows(activated, grad_low)
        dact = contract_cols(grad_low, down_weight[layer])
        sig = jax.nn.sigmoid(gate)
        dgate = (dact * up * sig * (1.0 + gate * (1.0 - sig))).astype(low)
        dup = (dact * gate * sig).astype(low)
        gate_up_grads[layer] = jnp.stack(
            [contract_rows(normed_two, dgate), contract_rows(normed_two, dup)]
        )
        dnormed_two = reduce_rows(
            contract_cols(dgate, gate_up_weight[layer, 0])
            + contract_cols(dup, gate_up_weight[layer, 1])
        )
        if layer == 0:
            early = (row_grads[1].astype(low), jnp.stack(gate_up_grads).astype(low))
            early = lax.psum(early + (jnp.stack(down_grads).astype(low),), "ctx")
        gain_two_grad, dmiddle = norm_backward(dnormed_two, middle, inv_two, gain_two)
        grad_mid = gradient + dmiddle
        mid_low = grad_mid.astype(low)
        out_part = contract_rows(att, mid_low)
        datt = contract_cols(mid_low, out_full[layer]).astype(low)
        delta = jnp.sum(
            (datt.astype(full) * weighted).reshape(own_rows, QUERY_HEADS, HEAD_SIZE), axis=-1
        )
        delta = delta.T.reshape(KEY_VALUE_HEADS, 1, -1)
        columns = query.shape[1]
        dquery, dkv = local_call(
            attend_backward_kernel,
            [
                ((KEY_VALUE_HEADS, HEAD_SIZE, columns), full),
                ((key_count, 2 * kv_width), low),
            ],
            query,
            heads_in(datt),
            key_value,
            key_pos,
            query_pos,
            log_total,
            delta,
        )
        dkv = links.reduce("core", dkv.reshape(2, -1, 2 * kv_width))
        dkv = links.reduce("wa", dkv.reshape(wa_count, -1, 2 * kv_width))
        dkv = links.reduce("z", dkv.reshape(z_count, -1, 2 * kv_width))
        dqkv = jnp.concatenate(
            [
                rope(heads_out(dquery, own_rows) * score_scale, QUERY_HEADS, -sine),
                rope(dkv[:, :kv_width], KEY_VALUE_HEADS, -sine),
                dkv[:, kv_width:],
            ],
            axis=-1,
        ).astype(low)
        qkv_part = contract_rows(normed, dqkv)
        dnormed = contract_cols(dqkv, qkv_full[layer])
        gain_one_grad, dinput = norm_backward(dnormed, layer_input, inv_one, gain_one)
        gradient = grad_mid + dinput
        if layer > 0:
            grad_low = gather_rows(gradient)
        block = jnp.concatenate([qkv_part, out_part], axis=1).astype(low)
        block = block.reshape(wa_count, -1, block.shape[1])
        gains = jnp.concatenate(
            [gain_one_grad, gain_two_grad, jnp.zeros((block.shape[2] - 2 * width,), full)]
        ).astype(low)
        pad_rows = 16 + (-block.shape[1]) % 16
        gains = jnp.broadcast_to(gains, (wa_count, pad_rows, gains.shape[0]))
        row_grads[layer] = links.reduce("wa", jnp.concatenate([block, gains], axis=1))
        if layer > 0:
            grad_low, row_grads[layer] = lax.optimization_barrier((grad_low, row_grads[layer]))
    ends = links.gather("wa", jnp.stack([hidden_own, gradient.astype(low)])).astype(full)
    hidden_out, input_grad = (ends[:, at].reshape(row_count, width) for at in range(2))
    rows_sum = jnp.stack([sum_over_ctx(links, row_grads[0]), early[0]]).astype(full)
    gate_up_sum = early[1].astype(full)
    down_sum = early[2].astype(full)
    return (
        hidden_out,
        input_grad,
        rows_sum[:, slab, :width],
        rows_sum[:, :slab, :qkv_cols],
        rows_sum[:, :slab, qkv_cols:],
        rows_sum[:, slab, width : 2 * width],
        gate_up_sum,
        down_sum,
    )


def solution(mesh):
    placed = (
        P("ctx", None),
        P(),
        P(),
        P(None, "wa", None),
        P(None, "wa", None),
        P(),
        P(None, None, None, "wa"),
        P(None, "wa", None),
        P("ctx", None),
    )
    return jax.shard_map(
        per_device,
        mesh=mesh,
        in_specs=placed,
        out_specs=(
            P("ctx", None),
            P("ctx", None),
            P(),
            P(None, "wa", None),
            P(None, "wa", None),
            P(),
            P(None, None, None, "wa"),
            P(None, "wa", None),
        ),
        check_vma=False,
    )
```
